128 devices in a mesh: layer: 32 (over z, x_hi, y), group: 4 (over x_lo, core).
Axes of the slice: x: 4 (x_hi: 2, x_lo: 2; x = x_hi * 2 + x_lo), y: 4, z: 4, core: 2. Of those that a mesh axis runs over, the one named last changes fastest.
Arguments:
- travelling_layer_entries: float32 [32, 4, 1024, 256], P('layer', 'group'), may hold values from -6 to 6
- arriving_clusters: float32 [4, 8, 1024, 256], P('group'), may hold values from -6 to 6
- travelling_cluster_position: int32 [32, 4], replicated, may hold values from 0 to 1
- arriving_cluster_position: int32 [4, 8], replicated, may hold values from 0 to 1
- adjacency_patches: bfloat16 [8, 48, 128, 128], P('group'), may hold values from -0.21875 to 0.21875
- patch_read_range: int32 [8, 48], P('group'), may hold values from 0 to 63
- patch_write_range: int32 [8, 48], P('group'), may hold values from 0 to 7
- outdated_layer_entries: bfloat16 [32, 8192, 256], P('layer'), may hold values from -6 to 6
- neighbour_mixing_matrix: bfloat16 [32, 256, 256], P('layer'), may hold values from -0.375 to 0.375
- rescale_factors: float32 [32, 256], P('layer'), may hold values from 0.5 to 1.5
- expand_matrix: bfloat16 [32, 256, 512], P('layer'), may hold values from -0.375 to 0.375
- contract_matrix: bfloat16 [32, 512, 256], P('layer'), may hold values from -0.25 to 0.25
Outputs:
- outputs: float32 [32, 4, 1024, 256], P('layer', 'group')
- history_out: bfloat16 [32, 8192, 256], P('layer')
The draws below stay inside these ranges and needn't reach their ends.
Inputs may be any that keep to these rules, and one draw needn't show every extreme that they name: `travelling_cluster_position`: local slot of a group within its stream. `arriving_cluster_position`: local slot of a new group within its stream. `patch_read_range`: row block of a layer's whole history.
All inputs are finite; a program needn't handle non-finite values.
Results may differ from the reference program's by a relative error of at most 0.0095.
Values may be sent and summed in bfloat16 or wider, within the bound.
No kernel may reach another device: no remote copies, remote signals or barrier semaphores. Data moves between devices by JAX's collectives and lax.ppermute only.
A program may use at most 128 MiB of HBM per device.

```python
import jax
import jax.numpy as jnp
from jax import lax

EMBED_BREADTH = 256
FF = 512
TB = 128
TILES = 48
STREAM_SLOTS = 2
CLUSTER_NODES = 1024
RELAY_BEATS = 8
NETWORK_DEPTH = 32
SLOTS = 8
HIST = 8192
BLOCKS = 64
NB = 8
N_GROUP = 4


def plant(values, own_key, low, top_value):
    longest = values.shape.index(max(values.shape))
    spots = []
    for shift in (0, 1):
        where = [jax.random.randint(jax.random.fold_in(own_key, axis), (), 0, length) for axis, length in enumerate(values.shape)]
        where[longest] = (where[longest] + shift) % values.shape[longest]
        spots.append(tuple(where))
    return values.at[spots[0]].set(low).at[spots[1]].set(top_value)


def levels(own_key, extent, shards, least, largest):
    def one(axis_at, parts):
        steps = jax.random.uniform(jax.random.fold_in(jax.random.fold_in(own_key, 6), axis_at), (parts,), jnp.float32, least / len(shards), largest / len(shards))
        return jnp.repeat(jnp.exp(steps), extent[axis_at] // parts).reshape((-1,) + (1,) * (len(extent) - axis_at - 1))

    loudness = one(*shards[0])
    for cut in shards[1:]:
        loudness = loudness * one(*cut)
    return loudness


def normal_values(key, shape, scale, limit, cuts=(), kind=jnp.bfloat16):
    loudness = levels(key, shape, cuts, -0.22, 0.18) if cuts else 1.0
    entries = jax.random.normal(key, shape, jnp.float32) * scale * loudness
    return jnp.minimum(jnp.maximum(entries, -limit), limit).astype(kind)


def setup_inputs(seed: int = 0) -> dict:
    streams_of = jax.random.split(jax.random.key(seed), 13)
    return {
        "travelling_layer_entries": normal_values(streams_of[0], (NETWORK_DEPTH, N_GROUP, CLUSTER_NODES, EMBED_BREADTH), 1.0, 6.0, ((0, 32), (1, 4)), jnp.float32),
        "arriving_clusters": normal_values(streams_of[1], (N_GROUP, RELAY_BEATS, CLUSTER_NODES, EMBED_BREADTH), 1.0, 6.0, ((0, 4),), jnp.float32),
        "travelling_cluster_position": plant(jax.random.randint(streams_of[2], (NETWORK_DEPTH, N_GROUP), 0, STREAM_SLOTS), jax.random.fold_in(streams_of[2], 1), 0, STREAM_SLOTS - 1).astype(jnp.int32),
        "arriving_cluster_position": plant(jax.random.randint(streams_of[3], (N_GROUP, RELAY_BEATS), 0, STREAM_SLOTS), jax.random.fold_in(streams_of[3], 1), 0, STREAM_SLOTS - 1).astype(jnp.int32),
        "adjacency_patches": normal_values(streams_of[4], (SLOTS, TILES, TB, TB), (TILES * TB * TB // CLUSTER_NODES) ** -0.5, 0.21875, ((0, 4),)),
        "patch_read_range": plant(jax.random.randint(streams_of[5], (SLOTS, TILES), 0, BLOCKS), jax.random.fold_in(streams_of[5], 1), 0, BLOCKS - 1).astype(jnp.int32),
        "patch_write_range": plant(jax.random.randint(streams_of[6], (SLOTS, TILES), 0, NB), jax.random.fold_in(streams_of[6], 1), 0, NB - 1).astype(jnp.int32),
        "outdated_layer_entries": normal_values(streams_of[7], (NETWORK_DEPTH, HIST, EMBED_BREADTH), 1.0, 6.0, ((0, 32),)),
        "neighbour_mixing_matrix": normal_values(streams_of[8], (NETWORK_DEPTH, EMBED_BREADTH, EMBED_BREADTH), EMBED_BREADTH ** -0.5, 0.375, ((0, 32),)),
        "rescale_factors": jnp.clip(0.5 + 1.0 * jax.random.uniform(streams_of[9], (NETWORK_DEPTH, EMBED_BREADTH), jnp.float32) ** levels(streams_of[9], (NETWORK_DEPTH, EMBED_BREADTH), ((0, 32),), -0.2, 0.2), 0.5, 1.5),
        "expand_matrix": normal_values(streams_of[10], (NETWORK_DEPTH, EMBED_BREADTH, FF), EMBED_BREADTH ** -0.5, 0.375, ((0, 32),)),
        "contract_matrix": normal_values(streams_of[11], (NETWORK_DEPTH, FF, EMBED_BREADTH), FF ** -0.5, 0.25, ((0, 32),)),
    }


def layer_rows(inputs, aggregated, conv_mat, norm_vec, up_mat, down_mat):
    convolved = jnp.dot(aggregated, conv_mat, preferred_element_type=jnp.float32)
    residual_sum = inputs + jax.nn.relu(convolved)
    scale = lax.rsqrt(lax.optimization_barrier(jnp.mean(residual_sum * residual_sum, axis=-1, keepdims=True)) + 1e-06)
    normed = (residual_sum * scale * norm_vec).astype(jnp.bfloat16)
    hidden = jax.nn.gelu(jnp.dot(normed, up_mat, preferred_element_type=jnp.float32)).astype(jnp.bfloat16)
    return residual_sum + jnp.dot(hidden, down_mat, preferred_element_type=jnp.float32)

def aggregate(history_now, tile_set, tile_from, tile_to):
    blocks = history_now.reshape(-1, TB, history_now.shape[-1])[tile_from]
    products = jnp.einsum('tij,tjd->tid', tile_set.astype(jnp.float32), blocks.astype(jnp.float32), precision=lax.Precision.HIGHEST)
    onehot = (tile_to[None, :] == jnp.arange(CLUSTER_NODES // TB, dtype=jnp.int32)[:, None]).astype(jnp.float32)
    summed = jnp.einsum('bt,tid->bid', onehot, products, precision=lax.Precision.HIGHEST)
    return summed.reshape(CLUSTER_NODES, -1).astype(jnp.bfloat16)

def reference(travelling_layer_entries, arriving_clusters, travelling_cluster_position, arriving_cluster_position, adjacency_patches, patch_read_range, patch_write_range, outdated_layer_entries, neighbour_mixing_matrix, rescale_factors, expand_matrix, contract_matrix):
    cluster_response_entries = travelling_layer_entries
    slot_lookup_table = travelling_cluster_position
    history_all = outdated_layer_entries

    def one_layer(packed):
        acts, history_slot_list, history_now, conv_mat, norm_vec, up_mat, down_mat = packed
        written = acts.astype(jnp.bfloat16)
        for group_stream in range(N_GROUP):
            global_slot_index = (group_stream * STREAM_SLOTS + history_slot_list[group_stream]).astype(jnp.int32)
            history_now = lax.dynamic_update_slice(history_now, written[group_stream], ((global_slot_index * CLUSTER_NODES).astype(jnp.int32), jnp.int32(0)))
        results = []
        for group_stream in range(N_GROUP):
            global_slot_index = (group_stream * STREAM_SLOTS + history_slot_list[group_stream]).astype(jnp.int32)
            aggregated = aggregate(history_now, adjacency_patches[global_slot_index], patch_read_range[global_slot_index], patch_write_range[global_slot_index])
            results.append(layer_rows(acts[group_stream], aggregated, conv_mat, norm_vec, up_mat, down_mat))
        return (jnp.stack(results), history_now)
    results = cluster_response_entries
    for beat_no in range(RELAY_BEATS):
        results, history_all = lax.map(one_layer, (cluster_response_entries, slot_lookup_table, history_all, neighbour_mixing_matrix, rescale_factors, expand_matrix, contract_matrix))
        if beat_no < RELAY_BEATS - 1:
            cluster_response_entries = jnp.concatenate([arriving_clusters[:, beat_no][None], results[:-1]], axis=0)
            slot_lookup_table = jnp.concatenate([arriving_cluster_position[:, beat_no][None], slot_lookup_table[:-1]], axis=0)
    return (results, history_all)
```

```python
import functools

import jax
import jax.numpy as jnp
from jax import lax
from jax.experimental import pallas as pl
from jax.experimental.pallas import tpu as pltpu
from jax.sharding import PartitionSpec as P

CHUNKS = 2
ROWS = 256
BF, F32, I32 = jnp.bfloat16, jnp.float32, jnp.int32
VMEM = pl.BlockSpec(memory_space=pltpu.VMEM)
SMEM = pl.BlockSpec(memory_space=pltpu.SMEM)
ANY = pl.BlockSpec(memory_space=pl.ANY)
PARAMS = dict(vmem_limit_bytes=40 * 1024 * 1024)


def prepare_kernel(tiles, nb, src_ref, dst_ref, hist_in, tile_in, sched, hist, tile_out, fill, sem):
    slots = src_ref.shape[0]
    pairs = (tiles + nb) // 2
    starts = 4 * pairs
    copies = [
        pltpu.make_async_copy(hist_in, hist, sem.at[0]),
        pltpu.make_async_copy(tile_in, tile_out.at[pl.ds(0, slots * tiles)], sem.at[1]),
    ]
    for copy in copies:
        copy.start()
    tile_out[slots * tiles] = jnp.zeros(tile_out.shape[1:], tile_out.dtype)
    for s in range(slots):
        for k in range(nb):
            fill[k] = 0

        def count(t, _):
            k = dst_ref[s, t]
            fill[k] = fill[k] + 1
            return 0

        lax.fori_loop(0, tiles, count, 0)

        def blank(i, _):
            sched[s, i] = slots * tiles
            sched[s, 2 * pairs + i] = 0
            return 0

        lax.fori_loop(0, 2 * pairs, blank, 0)
        first = jnp.int32(0)
        for k in range(nb):
            sched[s, starts + k] = first
            first = first + lax.div(fill[k] + 1, jnp.int32(2))
            fill[k] = 0
        sched[s, starts + nb] = first

        def place(t, _):
            k = dst_ref[s, t]
            at = 2 * sched[s, starts + k] + fill[k]
            fill[k] = fill[k] + 1
            sched[s, at] = s * tiles + t
            sched[s, 2 * pairs + at] = src_ref[s, t]
            @pl.when(lax.rem(at, jnp.int32(2)) == 0)
            def _():
                sched[s, 2 * pairs + at + 1] = src_ref[s, t]

            return 0

        lax.fori_loop(0, tiles, place, 0)
    for copy in copies:
        copy.wait()


def beat_kernel(first, last, nb, pairs, chunks, *refs):
    refs = list(refs)
    take = lambda n: [refs.pop(0) for _ in range(n)]
    scal, sched, hist_in, tiles, mixing, gain, expand, contract = take(8)
    parts = [take(chunks) for _ in range(4)]
    entry = take(1)[0] if first else None
    feed = None if last else take(1)[0]
    if last:
        result, hist_out = take(2)
        hist = hist_in
    else:
        results = take(chunks)
        hist = take(1)[0]
    prods, sems = take(2)
    per = nb // chunks
    own = scal[4]
    swap = scal[5]
    feeds = scal[6] == 1
    slot_of = lambda c: (c * 2 + scal[c]) * nb
    loads = []
    for i, part in enumerate(parts):
        base = slot_of(own ^ i ^ swap)
        for k in range(chunks):
            loads.append(
                pltpu.make_async_copy(part[k], hist.at[pl.ds(base + k * per, per)], sems.at[i * chunks + k])
            )
    for copy in loads:
        copy.start()
    if not last:
        arrivals = [
            pltpu.make_async_copy(feed.at[pl.ds(k * per, per)], results[k], sems.at[4 * chunks + k])
            for k in range(chunks)
        ]

        @pl.when(feeds)
        def _():
            for copy in arrivals:
                copy.start()

    for copy in loads:
        copy.wait()
    if last:
        leave = pltpu.make_async_copy(hist, hist_out, sems.at[4 * chunks])
        leave.start()
    mine = scal[own]
    for p in range(pairs):
        left = jnp.concatenate([tiles[sched[mine, 2 * p]], tiles[sched[mine, 2 * p + 1]]], axis=1)
        right = jnp.concatenate(
            [hist[sched[mine, 2 * pairs + 2 * p]], hist[sched[mine, 2 * pairs + 2 * p + 1]]], axis=0
        )
        prods[p] = jnp.dot(left, right, preferred_element_type=F32)
    width = prods.shape[2]
    tb = prods.shape[1]
    own_base = slot_of(own)
    step = ROWS // tb
    for r in range(nb // step):
        pieces = []
        for k in range(r * step, (r + 1) * step):
            pieces.append(
                lax.fori_loop(
                    sched[mine, 4 * pairs + k],
                    sched[mine, 4 * pairs + k + 1],
                    lambda p, acc: acc + prods[p],
                    jnp.zeros((tb, width), F32),
                ).astype(BF)
            )
        aggregated = jnp.concatenate(pieces, axis=0)
        if first:
            inputs = entry[pl.ds(r * step, step)].reshape(ROWS, width)
        else:
            inputs = hist[pl.ds(own_base + r * step, step)].reshape(ROWS, width).astype(F32)
        mixed = inputs + jax.nn.relu(jnp.dot(aggregated, mixing[...], preferred_element_type=F32))
        scale = lax.rsqrt(jnp.mean(mixed * mixed, axis=-1, keepdims=True) + 1e-06)
        normed = (mixed * scale * gain[...]).astype(BF)
        hidden = jax.nn.gelu(jnp.dot(normed, expand[...], preferred_element_type=F32)).astype(BF)
        out = mixed + jnp.dot(hidden, contract[...], preferred_element_type=F32)
        out = out.reshape(step, tb, width)
        if last:
            result[pl.ds(r * step, step)] = out
        else:
            k, at = divmod(r * step, per)

            @pl.when(jnp.logical_not(feeds))
            def _():
                results[k][pl.ds(at, step)] = out.astype(BF)

    if last:
        leave.wait()
    else:

        @pl.when(feeds)
        def _():
            for copy in arrivals:
                copy.wait()


def local(
    travelling_layer_entries,
    arriving_clusters,
    travelling_cluster_position,
    arriving_cluster_position,
    adjacency_patches,
    patch_read_range,
    patch_write_range,
    outdated_layer_entries,
    neighbour_mixing_matrix,
    rescale_factors,
    expand_matrix,
    contract_matrix,
):
    layers, streams = lax.axis_size("layer"), lax.axis_size("group")
    layer, group = lax.axis_index("layer"), lax.axis_index("group")
    slots, tiles, tb, _ = adjacency_patches.shape
    beats = arriving_clusters.shape[1]
    rows, width = travelling_layer_entries.shape[2:]
    nb = rows // tb
    per = nb // CHUNKS
    blocks = outdated_layer_entries.shape[1] // tb
    pairs = (tiles + nb) // 2
    sched_len = -(-(4 * pairs + nb + 1) // 128) * 128

    sched, hist, tile_set = pl.pallas_call(
        functools.partial(prepare_kernel, tiles, nb),
        out_shape=(
            jax.ShapeDtypeStruct((slots, sched_len), I32),
            pltpu.VMEM((blocks, tb, width), BF),
            pltpu.VMEM((slots * tiles + 1, tb, tb), BF),
        ),
        in_specs=[SMEM, SMEM, ANY, ANY],
        out_specs=(SMEM, VMEM, VMEM),
        scratch_shapes=[pltpu.SMEM((nb,), I32), pltpu.SemaphoreType.DMA((2,))],
        compiler_params=pltpu.CompilerParams(**PARAMS),
    )(
        patch_read_range,
        patch_write_range,
        outdated_layer_entries[0].reshape(blocks, tb, width),
        adjacency_patches.reshape(slots * tiles, tb, tb),
    )

    beat_ids = jnp.arange(beats)
    from_start = travelling_cluster_position[jnp.clip(layer - beat_ids, 0, layers - 1)]
    from_feed = arriving_cluster_position.T[jnp.clip(beat_ids - 1 - layer, 0, beats - 1)]
    slot_table = jnp.where((layer - beat_ids >= 0)[:, None], from_start, from_feed)
    wrapped = layer % 4 == 0
    swap = jnp.where((beat_ids > 0) & wrapped, 2, 0)
    scal = jnp.concatenate(
        [
            slot_table.astype(I32),
            jnp.full((beats, 1), group, I32),
            swap[:, None].astype(I32),
            jnp.full((beats, 1), layer == layers - 1, I32),
            jnp.zeros((beats, 1), I32),
        ],
        axis=1,
    )
    feed = arriving_clusters[0].astype(BF).reshape(beats, nb, tb, width)
    entry = travelling_layer_entries[0, 0].reshape(nb, tb, width)
    entry_bf = entry.astype(BF)

    chip_pairs = [(i, i ^ 2) for i in range(streams)]
    core_pairs = [(i, i ^ 1) for i in range(streams)]
    relay = [
        (l * streams + g, (l + 1) % layers * streams + (g ^ 2 if l % 4 == 3 else g))
        for l in range(layers)
        for g in range(streams)
    ]
    current = [entry_bf[k * per : (k + 1) * per] for k in range(CHUNKS)]
    for beat in range(beats):
        first, last = beat == 0, beat == beats - 1
        across = [lax.ppermute(part, "group", chip_pairs) for part in current]
        beside = [lax.ppermute(part, "group", core_pairs) for part in current]
        corner = [lax.ppermute(part, "group", core_pairs) for part in across]
        parts = [*current, *beside, *across, *corner]
        operands = [
            scal[beat], sched, hist, tile_set,
            neighbour_mixing_matrix[0], rescale_factors, expand_matrix[0], contract_matrix[0],
            *parts,
        ]
        specs = [SMEM, SMEM, VMEM, VMEM, VMEM, VMEM, VMEM, VMEM] + [ANY] * len(parts)
        if first:
            operands.append(entry)
            specs.append(VMEM)
        if not last:
            operands.append(feed[beat])
            specs.append(ANY)
        if last:
            shapes = (jax.ShapeDtypeStruct((nb, tb, width), F32), jax.ShapeDtypeStruct((blocks, tb, width), BF))
            out_specs, alias = (VMEM, ANY), {}
        else:
            shapes = (jax.ShapeDtypeStruct((per, tb, width), BF),) * CHUNKS + (pltpu.VMEM((blocks, tb, width), BF),)
            out_specs, alias = (VMEM,) * CHUNKS + (VMEM,), {2: CHUNKS}
        outs = pl.pallas_call(
            functools.partial(beat_kernel, first, last, nb, pairs, CHUNKS),
            out_shape=shapes,
            in_specs=specs,
            out_specs=out_specs,
            input_output_aliases=alias,
            scratch_shapes=[
                pltpu.VMEM((pairs, tb, width), F32),
                pltpu.SemaphoreType.DMA((5 * CHUNKS,)),
            ],
            compiler_params=pltpu.CompilerParams(**PARAMS),
            cost_estimate=pl.CostEstimate(flops=1_100_000_000, bytes_accessed=8_000_000, transcendentals=600_000),
        )(*operands)
        if last:
            result, history = outs
        else:
            hist = outs[-1]
            current = [lax.ppermute(part, ("layer", "group"), relay) for part in outs[:-1]]
    return (
        result.reshape(1, 1, rows, width),
        history.reshape(1, blocks * tb, width),
    )


def solution(mesh):
    return jax.shard_map(
        local,
        mesh=mesh,
        in_specs=(
            P("layer", "group", None, None),
            P("group", None, None, None),
            P(),
            P(),
            P("group", None, None, None),
            P("group", None),
            P("group", None),
            P("layer", None, None),
            P("layer", None, None),
            P("layer", None),
            P("layer", None, None),
            P("layer", None, None),
        ),
        out_specs=(P("layer", "group", None, None), P("layer", None, None)),
        check_vma=False,
    )
```

```python
import functools

import jax
import jax.numpy as jnp
from jax import lax
from jax.experimental import pallas as pl
from jax.experimental.pallas import tpu as pltpu
from jax.sharding import PartitionSpec as P

SIZES = (2, 2, 2, 2)
STEP = 4
WRAP, HOP, CHIP = 2, 0, 2
BF, F32, I32 = jnp.bfloat16, jnp.float32, jnp.int32
VMEM = pl.BlockSpec(memory_space=pltpu.VMEM)
SMEM = pl.BlockSpec(memory_space=pltpu.SMEM)
HBM = pl.BlockSpec(memory_space=pltpu.HBM)
ANY = pl.BlockSpec(memory_space=pl.ANY)
OFFSETS = tuple(sum(SIZES[:k]) for k in range(len(SIZES)))
CHUNKS = len(SIZES)
PARAMS = dict(vmem_limit_bytes=40 * 1024 * 1024)


def layer_rows(inputs, aggregated, mixing, gain, expand, contract):
    mixed = inputs + jax.nn.relu(jnp.dot(aggregated, mixing[...], preferred_element_type=F32))
    scale = lax.rsqrt(jnp.mean(mixed * mixed, axis=-1, keepdims=True) + 1e-06)
    normed = (mixed * scale * gain[...]).astype(BF)
    hidden = jax.nn.gelu(jnp.dot(normed, expand[...], preferred_element_type=F32)).astype(BF)
    return mixed + jnp.dot(hidden, contract[...], preferred_element_type=F32)


def beat_kernel(beat, last, nb, pairs, where, *refs):
    refs = list(refs)
    take = lambda n: [refs.pop(0) for _ in range(n)]
    scal, sched, hist_in, tiles, mixing, gain, expand, contract = take(8)
    parts = [(i, k, ref) for (i, k), ref in zip(where, take(len(where)))]
    entry = take(1)[0] if beat == 0 else None
    feed = None if last else take(1)[0]
    if last:
        result, hist_out = take(2)
        hist = hist_in
    else:
        results = take(CHUNKS)
        hist = take(1)[0]
    prods, aggs, sem = take(3)
    arrived = None if last else take(1)[0]
    tb, width = prods.shape[1:]
    own = scal[beat, 4]
    feeds = scal[beat, 6] == 1
    if beat == 0:
        stale = pltpu.make_async_copy(hist_in, hist, sem.at[1])
        stale.start()
    if not last:
        arrival = pltpu.make_async_copy(feed.at[beat], arrived, sem.at[0])

        @pl.when(feeds)
        def _():
            arrival.start()

    if beat == 0:
        stale.wait()
    for i, k, ref in parts:
        c = own ^ i ^ scal[beat, 5]
        base = (c * 2 + scal[beat, c]) * nb + OFFSETS[k]
        hist[pl.ds(base, SIZES[k])] = ref[...]
    if last:
        leave = pltpu.make_async_copy(hist, hist_out, sem.at[0])
        leave.start()

    def compute():
        mine = scal[beat, own]
        for p in range(pairs):
            second = sched[mine, 2 * p + 1]
            right = tiles[jnp.maximum(second, 0)]
            right = jnp.where(second >= 0, right, jnp.zeros_like(right))
            left = jnp.concatenate([tiles[sched[mine, 2 * p]], right], axis=1)
            rows = jnp.concatenate(
                [hist[sched[mine, 2 * pairs + 2 * p]], hist[sched[mine, 2 * pairs + 2 * p + 1]]], axis=0
            )
            prods[p] = jnp.dot(left, rows, preferred_element_type=F32)

        def block(k, _):
            aggs[k] = lax.fori_loop(
                sched[mine, 4 * pairs + k],
                sched[mine, 4 * pairs + k + 1],
                lambda p, acc: acc + prods[p],
                jnp.zeros((tb, width), F32),
            ).astype(BF)
            return 0

        lax.fori_loop(0, nb, block, 0)
        own_base = (own * 2 + mine) * nb
        for r in range(0, nb, STEP):
            if beat == 0:
                inputs = entry[pl.ds(r, STEP)]
            else:
                inputs = hist[pl.ds(own_base + r, STEP)].astype(F32)
            aggregated = aggs[pl.ds(r, STEP)].reshape(-1, width)
            out = layer_rows(inputs.reshape(-1, width), aggregated, mixing, gain, expand, contract)
            out = out.reshape(STEP, tb, width)
            if last:
                result[pl.ds(r, STEP)] = out
            else:
                for k, size in enumerate(SIZES):
                    low, high = max(r, OFFSETS[k]), min(r + STEP, OFFSETS[k] + size)
                    if low < high:
                        results[k][low - OFFSETS[k] : high - OFFSETS[k]] = out[low - r : high - r].astype(BF)

    if last:
        compute()
        leave.wait()
    else:
        pl.when(jnp.logical_not(feeds))(compute)

        @pl.when(feeds)
        def _():
            arrival.wait()
            for k, size in enumerate(SIZES):
                results[k][...] = arrived[pl.ds(OFFSETS[k], size)].astype(BF)


def local(
    travelling_layer_entries,
    arriving_clusters,
    travelling_cluster_position,
    arriving_cluster_position,
    adjacency_patches,
    patch_read_range,
    patch_write_range,
    outdated_layer_entries,
    neighbour_mixing_matrix,
    rescale_factors,
    expand_matrix,
    contract_matrix,
):
    layers, streams = lax.axis_size("layer"), lax.axis_size("group")
    layer, group = lax.axis_index("layer"), lax.axis_index("group")
    slots, tiles, tb, _ = adjacency_patches.shape
    beats = arriving_clusters.shape[1]
    rows, width = travelling_layer_entries.shape[2:]
    nb = rows // tb
    blocks = outdated_layer_entries.shape[1] // tb
    pairs = (tiles + nb) // 2
    beat_ids = jnp.arange(beats)
    started = jnp.arange(layers) == (layer - beat_ids)[:, None]
    fed = jnp.arange(beats) == (beat_ids - 1 - layer)[:, None]
    slot_table = jnp.sum(jnp.where(started[:, :, None], travelling_cluster_position, 0), axis=1)
    slot_table += jnp.sum(jnp.where(fed[:, None, :], arriving_cluster_position, 0), axis=2)
    wrapped = layer % 4 == 0
    swap = jnp.where(beat_ids > 0, jnp.where(wrapped, WRAP, HOP), 0)
    scal = jnp.concatenate(
        [
            slot_table.astype(I32),
            jnp.full((beats, 1), group, I32),
            swap[:, None].astype(I32),
            jnp.full((beats, 1), layer == layers - 1, I32),
            jnp.zeros((beats, 1), I32),
        ],
        axis=1,
    )
    ids, order, spots = jnp.arange(nb + 1), jnp.arange(tiles), jnp.arange(2 * pairs)
    members = patch_write_range[:, :, None] == ids[:nb]
    sized = (jnp.sum(members.astype(I32), axis=1) + 1) // 2
    begins = jnp.sum(jnp.where(ids[:nb] < ids[:, None], sized[:, None, :], 0), axis=2)
    rank = jnp.sum(
        (
            (patch_write_range[:, :, None] == patch_write_range[:, None, :])
            & (order[None, :] < order[:, None])
        ).astype(I32),
        axis=2,
    )
    place = 2 * jnp.sum(jnp.where(members, begins[:, None, :nb], 0), axis=2) + rank
    held = place[:, None, :] == spots[:, None]
    opens = place[:, None, :] == (spots // 2 * 2)[:, None]
    number = (jnp.arange(slots) * tiles)[:, None, None] + order + 1
    tile_at = jnp.sum(jnp.where(held, number, 0), axis=2) - 1
    own_read = jnp.sum(jnp.where(held, patch_read_range[:, None, :], 0), axis=2)
    first_read = jnp.sum(jnp.where(opens, patch_read_range[:, None, :], 0), axis=2)
    sched = jnp.concatenate(
        [
            jnp.where(spots % 2 == 0, jnp.maximum(tile_at, 0), tile_at),
            jnp.where(tile_at >= 0, own_read, first_read),
            begins,
        ],
        axis=1,
    ).astype(I32)
    feed = arriving_clusters[0].reshape(beats, nb, tb, width)
    entry = travelling_layer_entries[0, 0].reshape(nb, tb, width)
    hist = outdated_layer_entries[0].reshape(blocks, tb, width)
    tile_set = adjacency_patches.reshape(slots * tiles, tb, tb)
    weights = [neighbour_mixing_matrix[0], rescale_factors, expand_matrix[0], contract_matrix[0]]

    chip_pairs = [(i, i ^ CHIP) for i in range(streams)]
    core_pairs = [(i, i ^ 1) for i in range(streams)]
    relay = [
        (l * streams + g, (l + 1) % layers * streams + (g ^ (WRAP if l % 4 == 3 else HOP)))
        for l in range(layers)
        for g in range(streams)
    ]
    current = [entry[OFFSETS[k] : OFFSETS[k] + SIZES[k]].astype(BF) for k in range(CHUNKS)]
    where = [(i, k) for k in range(CHUNKS) for i in (0, 1, CHIP, CHIP ^ 1)]
    for beat in range(beats):
        last = beat == beats - 1
        parts = []
        for part in current:
            across = lax.ppermute(part, "group", chip_pairs)
            beside = lax.ppermute(part, "group", core_pairs)
            parts += [part, beside, across, lax.ppermute(across, "group", core_pairs)]
        operands = [scal, sched, hist, tile_set, *weights, *parts]
        specs = [SMEM] * 2 + [HBM if beat == 0 else VMEM] + [VMEM] * (5 + len(parts))
        scratch = [
            pltpu.VMEM((pairs, tb, width), F32),
            pltpu.VMEM((nb, tb, width), BF),
            pltpu.SemaphoreType.DMA((2,)),
        ]
        if beat == 0:
            operands.append(entry)
            specs.append(VMEM)
        if last:
            shapes = [jax.ShapeDtypeStruct((nb, tb, width), F32), jax.ShapeDtypeStruct((blocks, tb, width), BF)]
            out_specs, alias = [VMEM, ANY], {}
        else:
            operands.append(feed)
            specs.append(ANY)
            scratch.append(pltpu.VMEM((nb, tb, width), F32))
            shapes = [jax.ShapeDtypeStruct((size, tb, width), BF) for size in SIZES]
            shapes.append(pltpu.VMEM((blocks, tb, width), BF))
            out_specs, alias = [VMEM] * len(shapes), {2: CHUNKS} if beat else {}
        outs = pl.pallas_call(
            functools.partial(beat_kernel, beat, last, nb, pairs, where),
            out_shape=shapes,
            in_specs=specs,
            out_specs=out_specs,
            input_output_aliases=alias,
            scratch_shapes=scratch,
            compiler_params=pltpu.CompilerParams(**PARAMS),
            cost_estimate=pl.CostEstimate(flops=1_100_000_000, bytes_accessed=8_000_000, transcendentals=600_000),
        )(*operands)
        if last:
            result, history = outs
        else:
            hist = outs[-1]
            current = [lax.ppermute(part, ("layer", "group"), relay) for part in outs[:-1]]
    return (
        result.reshape(1, 1, rows, width),
        history.reshape(1, blocks * tb, width),
    )


def solution(mesh):
    return jax.shard_map(
        local,
        mesh=mesh,
        in_specs=(
            P("layer", "group", None, None),
            P("group", None, None, None),
            P(),
            P(),
            P("group", None, None, None),
            P("group", None),
            P("group", None),
            P("layer", None, None),
            P("layer", None, None),
            P("layer", None),
            P("layer", None, None),
            P("layer", None, None),
        ),
        out_specs=(P("layer", "group", None, None), P("layer", None, None)),
        check_vma=False,
    )
```

```python
import functools

import jax
import jax.numpy as jnp
from jax import lax
from jax.experimental import pallas as pl
from jax.experimental.pallas import tpu as pltpu
from jax.sharding import PartitionSpec as P

SIZES = (2, 2, 2, 2)
STEP = 4
COST = 140_000_000
STAGE = False
GATE = (2,)
WRAP, HOP, CHIP = 2, 0, 2
BF, F32, I32 = jnp.bfloat16, jnp.float32, jnp.int32
VMEM = pl.BlockSpec(memory_space=pltpu.VMEM)
SMEM = pl.BlockSpec(memory_space=pltpu.SMEM)
HBM = pl.BlockSpec(memory_space=pltpu.HBM)
ANY = pl.BlockSpec(memory_space=pl.ANY)
OFFSETS = tuple(sum(SIZES[:k]) for k in range(len(SIZES)))
CHUNKS = len(SIZES)
PARAMS = dict(vmem_limit_bytes=40 * 1024 * 1024)


def stage_kernel(*refs):
    sem = refs[-1]
    count = len(refs) // 2
    copies = [
        pltpu.make_async_copy(here, there, sem.at[n])
        for n, (here, there) in enumerate(zip(refs[:count], refs[count : 2 * count]))
    ]
    for copy in copies:
        copy.start()
    for copy in copies:
        copy.wait()


def layer_rows(inputs, aggregated, mixing, gain, expand, contract):
    mixed = inputs + jax.nn.relu(jnp.dot(aggregated, mixing[...], preferred_element_type=F32))
    scale = lax.rsqrt(jnp.mean(mixed * mixed, axis=-1, keepdims=True) + 1e-06)
    normed = (mixed * scale * gain[...]).astype(BF)
    hidden = jax.nn.gelu(jnp.dot(normed, expand[...], preferred_element_type=F32)).astype(BF)
    return mixed + jnp.dot(hidden, contract[...], preferred_element_type=F32)


def beat_kernel(beat, last, nb, pairs, where, chunks, *refs):
    refs = list(refs)
    take = lambda n: [refs.pop(0) for _ in range(n)]
    scal, sched, hist_in, tiles, mixing, gain, expand, contract = take(8)
    parts = [(i, k, ref) for (i, k), ref in zip(where, take(len(where)))]
    entry = take(1)[0] if beat == 0 else None
    feed = None if last else take(1)[0]
    if last:
        result, hist_out = take(2)
        hist = hist_in
    else:
        results = take(len(chunks))
        hist = take(1)[0] if parts else hist_in
    prods, aggs, sem = take(3)
    arrived = None if last else take(1)[0]
    tb, width = prods.shape[1:]
    low, high = OFFSETS[chunks[0]], OFFSETS[chunks[-1]] + SIZES[chunks[-1]]
    unroll = 4 if chunks == [0] else 7
    own = scal[beat, 4]
    feeds = scal[beat, 6] == 1
    if beat == 0 and parts:
        stale = pltpu.make_async_copy(hist_in, hist, sem.at[1])
        stale.start()
    if not last:
        arrival = pltpu.make_async_copy(feed.at[beat, pl.ds(low, high - low)], arrived, sem.at[0])

        @pl.when(feeds)
        def _():
            arrival.start()

    if beat == 0 and parts:
        stale.wait()
    for i, k, ref in parts:
        c = own ^ i ^ scal[beat, 5]
        base = (c * 2 + scal[beat, c]) * nb + OFFSETS[k]
        hist[pl.ds(base, SIZES[k])] = ref[...]
    if last:
        leave = pltpu.make_async_copy(hist, hist_out, sem.at[0])
        leave.start()

    def compute():
        mine = scal[beat, own]
        begin, end = sched[mine, 4 * pairs + low], sched[mine, 4 * pairs + high]

        def multiply(p):
            second = sched[mine, 2 * p + 1]
            right = tiles[jnp.maximum(second, 0)]
            right = jnp.where(second >= 0, right, jnp.zeros_like(right))
            left = jnp.concatenate([tiles[sched[mine, 2 * p]], right], axis=1)
            rows = jnp.concatenate(
                [hist[sched[mine, 2 * pairs + 2 * p]], hist[sched[mine, 2 * pairs + 2 * p + 1]]], axis=0
            )
            prods[p] = jnp.dot(left, rows, preferred_element_type=F32)

        def some(n, _):
            for j in range(unroll):
                multiply(jnp.minimum(begin + n * unroll + j, pairs - 1))
            return 0

        if last:
            for p in range(pairs):
                multiply(p)
        else:
            lax.fori_loop(0, lax.div(end - begin + unroll - 1, jnp.int32(unroll)), some, 0)

        def block(k, _):
            aggs[k] = lax.fori_loop(
                sched[mine, 4 * pairs + k],
                sched[mine, 4 * pairs + k + 1],
                lambda p, acc: acc + prods[p],
                jnp.zeros((tb, width), F32),
            ).astype(BF)
            return 0

        lax.fori_loop(low, high, block, 0)
        own_base = (own * 2 + mine) * nb
        steps = -(-(high - low) // STEP)
        bounds = [low + (high - low) * n // steps for n in range(steps + 1)]
        for r, end in zip(bounds, bounds[1:]):
            if beat == 0:
                inputs = entry[pl.ds(r, end - r)]
            else:
                inputs = hist[pl.ds(own_base + r, end - r)].astype(F32)
            aggregated = aggs[pl.ds(r, end - r)].reshape(-1, width)
            out = layer_rows(inputs.reshape(-1, width), aggregated, mixing, gain, expand, contract)
            out = out.reshape(end - r, tb, width)
            if last:
                result[pl.ds(r, end - r)] = out
                continue
            for k, ref in zip(chunks, results):
                top, stop = max(r, OFFSETS[k]), min(end, OFFSETS[k] + SIZES[k])
                if top < stop:
                    ref[top - OFFSETS[k] : stop - OFFSETS[k]] = out[top - r : stop - r].astype(BF)

    if last:
        compute()
        leave.wait()
    else:
        pl.when(jnp.logical_not(feeds))(compute)

        @pl.when(feeds)
        def _():
            arrival.wait()
            for k, ref in zip(chunks, results):
                ref[...] = arrived[pl.ds(OFFSETS[k] - low, SIZES[k])].astype(BF)


def local(
    travelling_layer_entries,
    arriving_clusters,
    travelling_cluster_position,
    arriving_cluster_position,
    adjacency_patches,
    patch_read_range,
    patch_write_range,
    outdated_layer_entries,
    neighbour_mixing_matrix,
    rescale_factors,
    expand_matrix,
    contract_matrix,
):
    layers, streams = lax.axis_size("layer"), lax.axis_size("group")
    layer, group = lax.axis_index("layer"), lax.axis_index("group")
    slots, tiles, tb, _ = adjacency_patches.shape
    beats = arriving_clusters.shape[1]
    rows, width = travelling_layer_entries.shape[2:]
    nb = rows // tb
    blocks = outdated_layer_entries.shape[1] // tb
    pairs = (tiles + nb) // 2
    beat_ids = jnp.arange(beats)
    started = jnp.arange(layers) == (layer - beat_ids)[:, None]
    fed = jnp.arange(beats) == (beat_ids - 1 - layer)[:, None]
    slot_table = jnp.sum(jnp.where(started[:, :, None], travelling_cluster_position, 0), axis=1)
    slot_table += jnp.sum(jnp.where(fed[:, None, :], arriving_cluster_position, 0), axis=2)
    wrapped = layer % 4 == 0
    swap = jnp.where(beat_ids > 0, jnp.where(wrapped, WRAP, HOP), 0)
    scal = jnp.concatenate(
        [
            slot_table.astype(I32),
            jnp.full((beats, 1), group, I32),
            swap[:, None].astype(I32),
            jnp.full((beats, 1), layer == layers - 1, I32),
            jnp.zeros((beats, 1), I32),
        ],
        axis=1,
    )
    ids, order, spots = jnp.arange(nb + 1), jnp.arange(tiles), jnp.arange(2 * pairs)
    members = patch_write_range[:, :, None] == ids[:nb]
    sized = (jnp.sum(members.astype(I32), axis=1) + 1) // 2
    begins = jnp.sum(jnp.where(ids[:nb] < ids[:, None], sized[:, None, :], 0), axis=2)
    rank = jnp.sum(
        (
            (patch_write_range[:, :, None] == patch_write_range[:, None, :])
            & (order[None, :] < order[:, None])
        ).astype(I32),
        axis=2,
    )
    place = 2 * jnp.sum(jnp.where(members, begins[:, None, :nb], 0), axis=2) + rank
    held = place[:, None, :] == spots[:, None]
    opens = place[:, None, :] == (spots // 2 * 2)[:, None]
    number = (jnp.arange(slots) * tiles)[:, None, None] + order + 1
    tile_at = jnp.sum(jnp.where(held, number, 0), axis=2) - 1
    own_read = jnp.sum(jnp.where(held, patch_read_range[:, None, :], 0), axis=2)
    first_read = jnp.sum(jnp.where(opens, patch_read_range[:, None, :], 0), axis=2)
    sched = jnp.concatenate(
        [
            jnp.where(spots % 2 == 0, jnp.maximum(tile_at, 0), tile_at),
            jnp.where(tile_at >= 0, own_read, first_read),
            begins,
        ],
        axis=1,
    ).astype(I32)
    feed = arriving_clusters[0].reshape(beats, nb, tb, width)
    entry = travelling_layer_entries[0, 0].reshape(nb, tb, width)
    hist = outdated_layer_entries[0].reshape(blocks, tb, width)
    tile_set = adjacency_patches.reshape(slots * tiles, tb, tb)
    kept = [tile_set, neighbour_mixing_matrix[0], rescale_factors, expand_matrix[0], contract_matrix[0], entry]
    if STAGE:
        kept = pl.pallas_call(
            stage_kernel,
            out_shape=[pltpu.VMEM(x.shape, x.dtype) for x in kept],
            in_specs=[HBM] * len(kept),
            out_specs=[VMEM] * len(kept),
            scratch_shapes=[pltpu.SemaphoreType.DMA((len(kept),))],
            compiler_params=pltpu.CompilerParams(**PARAMS),
            cost_estimate=pl.CostEstimate(flops=0, bytes_accessed=10_000_000, transcendentals=0),
        )(*kept)
    tile_set, *weights, staged = kept

    chip_pairs = [(i, i ^ CHIP) for i in range(streams)]
    core_pairs = [(i, i ^ 1) for i in range(streams)]
    relay = [
        (l * streams + g, (l + 1) % layers * streams + (g ^ (WRAP if l % 4 == 3 else HOP)))
        for l in range(layers)
        for g in range(streams)
    ]
    current = [entry[OFFSETS[k] : OFFSETS[k] + SIZES[k]].astype(BF) for k in range(CHUNKS)]
    for beat in range(beats):
        last = beat == beats - 1
        across = [lax.ppermute(part, "group", chip_pairs) for part in current]
        ready = lax.optimization_barrier((*current, *[across[k] for k in GATE]))
        beside = [lax.ppermute(part, "group", core_pairs) for part in ready[:CHUNKS]]
        settled = list(across)
        for k, part in zip(GATE, ready[CHUNKS:]):
            settled[k] = part
        corner = [lax.ppermute(part, "group", core_pairs) for part in settled]
        parts = [part for group_parts in zip(current, beside, across, corner) for part in group_parts]
        where = [(i, k) for k in range(CHUNKS) for i in (0, 1, CHIP, CHIP ^ 1)]

        def call(chunks, parts, hist):
            operands = [scal, sched, hist, tile_set, *weights, *parts]
            from_input = beat == 0 and parts
            specs = [SMEM] * 2 + [HBM if from_input else VMEM] + [VMEM] * (5 + len(parts))
            scratch = [
                pltpu.VMEM((pairs, tb, width), F32),
                pltpu.VMEM((nb, tb, width), BF),
                pltpu.SemaphoreType.DMA((2,)),
            ]
            if beat == 0:
                operands.append(staged)
                specs.append(VMEM)
            alias = {}
            share = sum(SIZES[k] for k in chunks)
            if last:
                shapes = [
                    jax.ShapeDtypeStruct((nb, tb, width), F32),
                    jax.ShapeDtypeStruct((blocks, tb, width), BF),
                ]
                out_specs = [VMEM, ANY]
            else:
                operands.append(feed)
                specs.append(ANY)
                scratch.append(pltpu.VMEM((share, tb, width), F32))
                shapes = [jax.ShapeDtypeStruct((SIZES[k], tb, width), BF) for k in chunks]
                if parts:
                    shapes.append(pltpu.VMEM((blocks, tb, width), BF))
                    alias = {} if from_input else {2: len(chunks)}
                out_specs = [VMEM] * len(shapes)
            return pl.pallas_call(
                functools.partial(beat_kernel, beat, last, nb, pairs, where if parts else [], chunks),
                out_shape=shapes,
                in_specs=specs,
                out_specs=out_specs,
                input_output_aliases=alias,
                scratch_shapes=scratch,
                compiler_params=pltpu.CompilerParams(**PARAMS),
                cost_estimate=pl.CostEstimate(
                    flops=share * COST, bytes_accessed=share * 1_000_000, transcendentals=share * 65536
                ),
            )(*operands)

        if last:
            result, history = call(list(range(CHUNKS)), parts, hist)
        else:
            front, hist = call([0], parts, hist)
            outs = [front, *call(list(range(1, CHUNKS)), [], hist)]
            current = [lax.ppermute(part, ("layer", "group"), relay) for part in outs]
    return (
        result.reshape(1, 1, rows, width),
        history.reshape(1, blocks * tb, width),
    )


def solution(mesh):
    return jax.shard_map(
        local,
        mesh=mesh,
        in_specs=(
            P("layer", "group", None, None),
            P("group", None, None, None),
            P(),
            P(),
            P("group", None, None, None),
            P("group", None),
            P("group", None),
            P("layer", None, None),
            P("layer", None, None),
            P("layer", None),
            P("layer", None, None),
            P("layer", None, None),
        ),
        out_specs=(P("layer", "group", None, None), P("layer", None, None)),
        check_vma=False,
    )
```

```python
import functools

import jax
import jax.numpy as jnp
from jax import lax
from jax.experimental import pallas as pl
from jax.experimental.pallas import tpu as pltpu
from jax.sharding import PartitionSpec as P

SIZES = (2, 2, 2, 2)
STEP = 4
COST = 140_000_000
GATE = (1, 2)
GATED = (2, 3)
WRAP, HOP, CHIP = 2, 0, 2
BF, F32, I32 = jnp.bfloat16, jnp.float32, jnp.int32
VMEM = pl.BlockSpec(memory_space=pltpu.VMEM)
SMEM = pl.BlockSpec(memory_space=pltpu.SMEM)
HBM = pl.BlockSpec(memory_space=pltpu.HBM)
ANY = pl.BlockSpec(memory_space=pl.ANY)
OFFSETS = tuple(sum(SIZES[:k]) for k in range(len(SIZES)))
CHUNKS = len(SIZES)
PARAMS = dict(vmem_limit_bytes=40 * 1024 * 1024)


def layer_rows(inputs, aggregated, mixing, gain, expand, contract):
    mixed = inputs + jax.nn.relu(jnp.dot(aggregated, mixing[...], preferred_element_type=F32))
    scale = lax.rsqrt(jnp.mean(mixed * mixed, axis=-1, keepdims=True) + 1e-06)
    normed = (mixed * scale * gain[...]).astype(BF)
    hidden = jax.nn.gelu(jnp.dot(normed, expand[...], preferred_element_type=F32)).astype(BF)
    return mixed + jnp.dot(hidden, contract[...], preferred_element_type=F32)


def beat_kernel(beat, last, nb, pairs, where, chunks, *refs):
    refs = list(refs)
    take = lambda n: [refs.pop(0) for _ in range(n)]
    scal, sched, hist_in, tiles, mixing, gain, expand, contract = take(8)
    parts = [(i, k, ref) for (i, k), ref in zip(where, take(len(where)))]
    entry = take(1)[0] if beat == 0 else None
    feed = None if last else take(1)[0]
    if last:
        result, hist_out = take(2)
        hist = hist_in
    else:
        results = take(len(chunks))
        hist = take(1)[0] if parts else hist_in
        if beat == 0 and parts:
            sources = [tiles, mixing, gain, expand, contract, entry]
            tiles, mixing, gain, expand, contract, entry = copied = take(6)
    prods, aggs, sem = take(3)
    arrived = None if last else take(1)[0]
    tb, width = prods.shape[1:]
    low, high = OFFSETS[chunks[0]], OFFSETS[chunks[-1]] + SIZES[chunks[-1]]
    unroll = 4 if chunks == [0] else 7
    own = scal[beat, 4]
    feeds = scal[beat, 6] == 1
    if beat == 0 and parts:
        stale = [pltpu.make_async_copy(hist_in, hist, sem.at[1])]
        for n, (here, there) in enumerate(zip(sources, copied)):
            stale.append(pltpu.make_async_copy(here, there, sem.at[2 + n]))
        for copy in stale:
            copy.start()
    if not last:
        arrival = pltpu.make_async_copy(feed.at[beat, pl.ds(low, high - low)], arrived, sem.at[0])

        @pl.when(feeds)
        def _():
            arrival.start()

    if beat == 0 and parts:
        for copy in stale:
            copy.wait()
    for i, k, ref in parts:
        c = own ^ i ^ scal[beat, 5]
        base = (c * 2 + scal[beat, c]) * nb + OFFSETS[k]
        hist[pl.ds(base, SIZES[k])] = ref[...]
    if last:
        leave = pltpu.make_async_copy(hist, hist_out, sem.at[0])
        leave.start()

    def compute():
        mine = scal[beat, own]
        begin, end = sched[mine, 4 * pairs + low], sched[mine, 4 * pairs + high]

        def multiply(p):
            second = sched[mine, 2 * p + 1]
            right = tiles[jnp.maximum(second, 0)]
            right = jnp.where(second >= 0, right, jnp.zeros_like(right))
            left = jnp.concatenate([tiles[sched[mine, 2 * p]], right], axis=1)
            rows = jnp.concatenate(
                [hist[sched[mine, 2 * pairs + 2 * p]], hist[sched[mine, 2 * pairs + 2 * p + 1]]], axis=0
            )
            prods[p] = jnp.dot(left, rows, preferred_element_type=F32)

        def some(n, _):
            for j in range(unroll):
                multiply(jnp.minimum(begin + n * unroll + j, pairs - 1))
            return 0

        if last:
            for p in range(pairs):
                multiply(p)
        else:
            lax.fori_loop(0, lax.div(end - begin + unroll - 1, jnp.int32(unroll)), some, 0)

        def block(k, _):
            aggs[k] = lax.fori_loop(
                sched[mine, 4 * pairs + k],
                sched[mine, 4 * pairs + k + 1],
                lambda p, acc: acc + prods[p],
                jnp.zeros((tb, width), F32),
            ).astype(BF)
            return 0

        lax.fori_loop(low, high, block, 0)
        own_base = (own * 2 + mine) * nb
        steps = -(-(high - low) // STEP)
        bounds = [low + (high - low) * n // steps for n in range(steps + 1)]
        for r, end in zip(bounds, bounds[1:]):
            if beat == 0:
                inputs = entry[pl.ds(r, end - r)]
            else:
                inputs = hist[pl.ds(own_base + r, end - r)].astype(F32)
            aggregated = aggs[pl.ds(r, end - r)].reshape(-1, width)
            out = layer_rows(inputs.reshape(-1, width), aggregated, mixing, gain, expand, contract)
            out = out.reshape(end - r, tb, width)
            if last:
                result[pl.ds(r, end - r)] = out
                continue
            for k, ref in zip(chunks, results):
                top, stop = max(r, OFFSETS[k]), min(end, OFFSETS[k] + SIZES[k])
                if top < stop:
                    ref[top - OFFSETS[k] : stop - OFFSETS[k]] = out[top - r : stop - r].astype(BF)

    if last:
        compute()
        leave.wait()
    else:
        pl.when(jnp.logical_not(feeds))(compute)

        @pl.when(feeds)
        def _():
            arrival.wait()
            for k, ref in zip(chunks, results):
                ref[...] = arrived[pl.ds(OFFSETS[k] - low, SIZES[k])].astype(BF)


def local(
    travelling_layer_entries,
    arriving_clusters,
    travelling_cluster_position,
    arriving_cluster_position,
    adjacency_patches,
    patch_read_range,
    patch_write_range,
    outdated_layer_entries,
    neighbour_mixing_matrix,
    rescale_factors,
    expand_matrix,
    contract_matrix,
):
    layers, streams = lax.axis_size("layer"), lax.axis_size("group")
    layer, group = lax.axis_index("layer"), lax.axis_index("group")
    slots, tiles, tb, _ = adjacency_patches.shape
    beats = arriving_clusters.shape[1]
    rows, width = travelling_layer_entries.shape[2:]
    nb = rows // tb
    blocks = outdated_layer_entries.shape[1] // tb
    pairs = (tiles + nb) // 2
    beat_ids = jnp.arange(beats)
    started = jnp.arange(layers) == (layer - beat_ids)[:, None]
    fed = jnp.arange(beats) == (beat_ids - 1 - layer)[:, None]
    slot_table = jnp.sum(jnp.where(started[:, :, None], travelling_cluster_position, 0), axis=1)
    slot_table += jnp.sum(jnp.where(fed[:, None, :], arriving_cluster_position, 0), axis=2)
    wrapped = layer % 4 == 0
    swap = jnp.where(beat_ids > 0, jnp.where(wrapped, WRAP, HOP), 0)
    scal = jnp.concatenate(
        [
            slot_table.astype(I32),
            jnp.full((beats, 1), group, I32),
            swap[:, None].astype(I32),
            jnp.full((beats, 1), layer == layers - 1, I32),
            jnp.zeros((beats, 1), I32),
        ],
        axis=1,
    )
    ids, order, spots = jnp.arange(nb + 1), jnp.arange(tiles), jnp.arange(2 * pairs)
    members = patch_write_range[:, :, None] == ids[:nb]
    sized = (jnp.sum(members.astype(I32), axis=1) + 1) // 2
    begins = jnp.sum(jnp.where(ids[:nb] < ids[:, None], sized[:, None, :], 0), axis=2)
    rank = jnp.sum(
        (
            (patch_write_range[:, :, None] == patch_write_range[:, None, :])
            & (order[None, :] < order[:, None])
        ).astype(I32),
        axis=2,
    )
    place = 2 * jnp.sum(jnp.where(members, begins[:, None, :nb], 0), axis=2) + rank
    held = place[:, None, :] == spots[:, None]
    opens = place[:, None, :] == (spots // 2 * 2)[:, None]
    number = (jnp.arange(slots) * tiles)[:, None, None] + order + 1
    tile_at = jnp.sum(jnp.where(held, number, 0), axis=2) - 1
    own_read = jnp.sum(jnp.where(held, patch_read_range[:, None, :], 0), axis=2)
    first_read = jnp.sum(jnp.where(opens, patch_read_range[:, None, :], 0), axis=2)
    sched = jnp.concatenate(
        [
            jnp.where(spots % 2 == 0, jnp.maximum(tile_at, 0), tile_at),
            jnp.where(tile_at >= 0, own_read, first_read),
            begins,
        ],
        axis=1,
    ).astype(I32)
    feed = arriving_clusters[0].reshape(beats, nb, tb, width)
    entry = travelling_layer_entries[0, 0].reshape(nb, tb, width)
    hist = outdated_layer_entries[0].reshape(blocks, tb, width)
    tile_set = adjacency_patches.reshape(slots * tiles, tb, tb)
    tile_set, *weights, staged = kept = [
        tile_set, neighbour_mixing_matrix[0], rescale_factors, expand_matrix[0], contract_matrix[0], entry
    ]

    chip_pairs = [(i, i ^ CHIP) for i in range(streams)]
    core_pairs = [(i, i ^ 1) for i in range(streams)]
    relay = [
        (l * streams + g, (l + 1) % layers * streams + (g ^ (WRAP if l % 4 == 3 else HOP)))
        for l in range(layers)
        for g in range(streams)
    ]
    current = [entry[OFFSETS[k] : OFFSETS[k] + SIZES[k]].astype(BF) for k in range(CHUNKS)]
    for beat in range(beats):
        last = beat == beats - 1
        across = [lax.ppermute(part, "group", chip_pairs) for part in current]
        ready = lax.optimization_barrier((*current, *[across[k] for k in GATE]))
        beside = [
            lax.ppermute((ready if k in GATED else current)[k], "group", core_pairs) for k in range(CHUNKS)
        ]
        settled = list(across)
        for k, part in zip(GATE, ready[CHUNKS:]):
            settled[k] = part
        corner = [lax.ppermute(part, "group", core_pairs) for part in settled]
        parts = [part for group_parts in zip(current, beside, across, corner) for part in group_parts]
        where = [(i, k) for k in range(CHUNKS) for i in (0, 1, CHIP, CHIP ^ 1)]

        def call(chunks, parts, hist):
            operands = [scal, sched, hist, tile_set, *weights, *parts]
            from_input = beat == 0 and parts
            first = HBM if from_input else VMEM
            specs = [SMEM] * 2 + [first] * 6 + [VMEM] * len(parts)
            scratch = [
                pltpu.VMEM((pairs, tb, width), F32),
                pltpu.VMEM((nb, tb, width), BF),
                pltpu.SemaphoreType.DMA((8,)),
            ]
            if beat == 0:
                operands.append(staged)
                specs.append(first)
            alias = {}
            share = sum(SIZES[k] for k in chunks)
            if last:
                shapes = [
                    jax.ShapeDtypeStruct((nb, tb, width), F32),
                    jax.ShapeDtypeStruct((blocks, tb, width), BF),
                ]
                out_specs = [VMEM, ANY]
            else:
                operands.append(feed)
                specs.append(ANY)
                scratch.append(pltpu.VMEM((share, tb, width), F32))
                shapes = [jax.ShapeDtypeStruct((SIZES[k], tb, width), BF) for k in chunks]
                if parts:
                    shapes.append(pltpu.VMEM((blocks, tb, width), BF))
                    alias = {} if from_input else {2: len(chunks)}
                if from_input:
                    shapes += [pltpu.VMEM(x.shape, x.dtype) for x in kept]
                out_specs = [VMEM] * len(shapes)
            return pl.pallas_call(
                functools.partial(beat_kernel, beat, last, nb, pairs, where if parts else [], chunks),
                out_shape=shapes,
                in_specs=specs,
                out_specs=out_specs,
                input_output_aliases=alias,
                scratch_shapes=scratch,
                compiler_params=pltpu.CompilerParams(**PARAMS),
                cost_estimate=pl.CostEstimate(
                    flops=share * COST, bytes_accessed=share * 1_000_000, transcendentals=share * 65536
                ),
            )(*operands)

        if last:
            result, history = call(list(range(CHUNKS)), parts, hist)
        else:
            front, hist, *handed = call([0], parts, hist)
            if beat == 0:
                tile_set, *weights, staged = handed
            outs = [front, *call(list(range(1, CHUNKS)), [], hist)]
            current = [lax.ppermute(part, ("layer", "group"), relay) for part in outs]
    return (
        result.reshape(1, 1, rows, width),
        history.reshape(1, blocks * tb, width),
    )


def solution(mesh):
    return jax.shard_map(
        local,
        mesh=mesh,
        in_specs=(
            P("layer", "group", None, None),
            P("group", None, None, None),
            P(),
            P(),
            P("group", None, None, None),
            P("group", None),
            P("group", None),
            P("layer", None, None),
            P("layer", None, None),
            P("layer", None),
            P("layer", None, None),
            P("layer", None, None),
        ),
        out_specs=(P("layer", "group", None, None), P("layer", None, None)),
        check_vma=False,
    )
```

```python
import functools

import jax
import jax.numpy as jnp
from jax import lax
from jax.experimental import pallas as pl
from jax.experimental.pallas import tpu as pltpu
from jax.sharding import PartitionSpec as P

SIZES = (2, 2, 2, 2)
STEP = 4
COST = 140_000_000
GATE = (1, 2)
GATED = (2, 3)
WRAP, HOP, CHIP = 2, 0, 2
BF, F32, I32 = jnp.bfloat16, jnp.float32, jnp.int32
VMEM = pl.BlockSpec(memory_space=pltpu.VMEM)
SMEM = pl.BlockSpec(memory_space=pltpu.SMEM)
HBM = pl.BlockSpec(memory_space=pltpu.HBM)
ANY = pl.BlockSpec(memory_space=pl.ANY)
OFFSETS = tuple(sum(SIZES[:k]) for k in range(len(SIZES)))
CHUNKS = len(SIZES)
PARAMS = dict(vmem_limit_bytes=40 * 1024 * 1024)


def layer_rows(inputs, aggregated, mixing, gain, expand, contract):
    mixed = inputs + jax.nn.relu(jnp.dot(aggregated, mixing[...], preferred_element_type=F32))
    scale = lax.rsqrt(jnp.mean(mixed * mixed, axis=-1, keepdims=True) + 1e-06)
    normed = (mixed * scale * gain[...]).astype(BF)
    hidden = jax.nn.gelu(jnp.dot(normed, expand[...], preferred_element_type=F32)).astype(BF)
    return mixed + jnp.dot(hidden, contract[...], preferred_element_type=F32)


def beat_kernel(beat, last, nb, pairs, where, chunks, *refs):
    refs = list(refs)
    take = lambda n: [refs.pop(0) for _ in range(n)]
    scal, sched, hist_in, tiles, mixing, gain, expand, contract = take(8)
    parts = [(i, k, ref) for (i, k), ref in zip(where, take(len(where)))]
    entry = take(1)[0] if beat == 0 else None
    feed = None if last else take(1)[0]
    if last:
        result, hist_out = take(2)
        hist = hist_in
    else:
        results = take(len(chunks))
        hist = take(1)[0] if parts else hist_in
        if beat == 0 and parts:
            sources = [tiles, mixing, gain, expand, contract, entry]
            tiles, mixing, gain, expand, contract, entry = copied = take(6)
    prods, aggs, sem = take(3)
    arrived = None if last else take(1)[0]
    tb, width = prods.shape[1:]
    low, high = OFFSETS[chunks[0]], OFFSETS[chunks[-1]] + SIZES[chunks[-1]]
    unroll = 4
    own = scal[beat, 4]
    feeds = scal[beat, 6] == 1
    if beat == 0 and parts:
        stale = [pltpu.make_async_copy(hist_in, hist, sem.at[1])]
        for n, (here, there) in enumerate(zip(sources, copied)):
            stale.append(pltpu.make_async_copy(here, there, sem.at[2 + n]))
        for copy in stale:
            copy.start()
    if not last:
        arrival = pltpu.make_async_copy(feed.at[beat, pl.ds(low, high - low)], arrived, sem.at[0])

        @pl.when(feeds)
        def _():
            arrival.start()

    if beat == 0 and parts:
        for copy in stale:
            copy.wait()
    for i, k, ref in parts:
        c = own ^ i ^ scal[beat, 5]
        base = (c * 2 + scal[beat, c]) * nb + OFFSETS[k]
        hist[pl.ds(base, SIZES[k])] = ref[...]
    if last:
        leave = pltpu.make_async_copy(hist, hist_out, sem.at[0])
        leave.start()

    def compute():
        mine = scal[beat, own]
        begin, end = sched[mine, 4 * pairs + low], sched[mine, 4 * pairs + high]

        def multiply(p):
            second = sched[mine, 2 * p + 1]
            right = tiles[jnp.maximum(second, 0)]
            right = jnp.where(second >= 0, right, jnp.zeros_like(right))
            left = jnp.concatenate([tiles[sched[mine, 2 * p]], right], axis=1)
            rows = jnp.concatenate(
                [hist[sched[mine, 2 * pairs + 2 * p]], hist[sched[mine, 2 * pairs + 2 * p + 1]]], axis=0
            )
            prods[p] = jnp.dot(left, rows, preferred_element_type=F32)

        def some(n, _):
            for j in range(unroll):
                multiply(jnp.minimum(begin + n * unroll + j, pairs - 1))
            return 0

        if chunks != [0]:
            for p in range(pairs):
                multiply(p)
        else:
            lax.fori_loop(0, lax.div(end - begin + unroll - 1, jnp.int32(unroll)), some, 0)

        def block(k, _):
            aggs[k] = lax.fori_loop(
                sched[mine, 4 * pairs + k],
                sched[mine, 4 * pairs + k + 1],
                lambda p, acc: acc + prods[p],
                jnp.zeros((tb, width), F32),
            ).astype(BF)
            return 0

        lax.fori_loop(low, high, block, 0)
        own_base = (own * 2 + mine) * nb
        steps = -(-(high - low) // STEP)
        bounds = [low + (high - low) * n // steps for n in range(steps + 1)]
        for r, end in zip(bounds, bounds[1:]):
            if beat == 0:
                inputs = entry[pl.ds(r, end - r)]
            else:
                inputs = hist[pl.ds(own_base + r, end - r)].astype(F32)
            aggregated = aggs[pl.ds(r, end - r)].reshape(-1, width)
            out = layer_rows(inputs.reshape(-1, width), aggregated, mixing, gain, expand, contract)
            out = out.reshape(end - r, tb, width)
            if last:
                result[pl.ds(r, end - r)] = out
                continue
            for k, ref in zip(chunks, results):
                top, stop = max(r, OFFSETS[k]), min(end, OFFSETS[k] + SIZES[k])
                if top < stop:
                    ref[top - OFFSETS[k] : stop - OFFSETS[k]] = out[top - r : stop - r].astype(BF)

    if last:
        compute()
        leave.wait()
    else:
        pl.when(jnp.logical_not(feeds))(compute)

        @pl.when(feeds)
        def _():
            arrival.wait()
            for k, ref in zip(chunks, results):
                ref[...] = arrived[pl.ds(OFFSETS[k] - low, SIZES[k])].astype(BF)


def local(
    travelling_layer_entries,
    arriving_clusters,
    travelling_cluster_position,
    arriving_cluster_position,
    adjacency_patches,
    patch_read_range,
    patch_write_range,
    outdated_layer_entries,
    neighbour_mixing_matrix,
    rescale_factors,
    expand_matrix,
    contract_matrix,
):
    layers, streams = lax.axis_size("layer"), lax.axis_size("group")
    layer, group = lax.axis_index("layer"), lax.axis_index("group")
    slots, tiles, tb, _ = adjacency_patches.shape
    beats = arriving_clusters.shape[1]
    rows, width = travelling_layer_entries.shape[2:]
    nb = rows // tb
    blocks = outdated_layer_entries.shape[1] // tb
    pairs = (tiles + nb) // 2
    beat_ids = jnp.arange(beats)
    started = jnp.arange(layers) == (layer - beat_ids)[:, None]
    fed = jnp.arange(beats) == (beat_ids - 1 - layer)[:, None]
    slot_table = jnp.sum(jnp.where(started[:, :, None], travelling_cluster_position, 0), axis=1)
    slot_table += jnp.sum(jnp.where(fed[:, None, :], arriving_cluster_position, 0), axis=2)
    wrapped = layer % 4 == 0
    swap = jnp.where(beat_ids > 0, jnp.where(wrapped, WRAP, HOP), 0)
    scal = jnp.concatenate(
        [
            slot_table.astype(I32),
            jnp.full((beats, 1), group, I32),
            swap[:, None].astype(I32),
            jnp.full((beats, 1), layer == layers - 1, I32),
            jnp.zeros((beats, 1), I32),
        ],
        axis=1,
    )
    ids, order, spots = jnp.arange(nb + 1), jnp.arange(tiles), jnp.arange(2 * pairs)
    members = patch_write_range[:, :, None] == ids[:nb]
    sized = (jnp.sum(members.astype(I32), axis=1) + 1) // 2
    begins = jnp.sum(jnp.where(ids[:nb] < ids[:, None], sized[:, None, :], 0), axis=2)
    rank = jnp.sum(
        (
            (patch_write_range[:, :, None] == patch_write_range[:, None, :])
            & (order[None, :] < order[:, None])
        ).astype(I32),
        axis=2,
    )
    place = 2 * jnp.sum(jnp.where(members, begins[:, None, :nb], 0), axis=2) + rank
    held = place[:, None, :] == spots[:, None]
    opens = place[:, None, :] == (spots // 2 * 2)[:, None]
    number = (jnp.arange(slots) * tiles)[:, None, None] + order + 1
    tile_at = jnp.sum(jnp.where(held, number, 0), axis=2) - 1
    own_read = jnp.sum(jnp.where(held, patch_read_range[:, None, :], 0), axis=2)
    first_read = jnp.sum(jnp.where(opens, patch_read_range[:, None, :], 0), axis=2)
    sched = jnp.concatenate(
        [
            jnp.where(spots % 2 == 0, jnp.maximum(tile_at, 0), tile_at),
            jnp.where(tile_at >= 0, own_read, first_read),
            begins,
        ],
        axis=1,
    ).astype(I32)
    feed = arriving_clusters[0].reshape(beats, nb, tb, width)
    entry = travelling_layer_entries[0, 0].reshape(nb, tb, width)
    hist = outdated_layer_entries[0].reshape(blocks, tb, width)
    tile_set = adjacency_patches.reshape(slots * tiles, tb, tb)
    tile_set, *weights, staged = kept = [
        tile_set, neighbour_mixing_matrix[0], rescale_factors, expand_matrix[0], contract_matrix[0], entry
    ]

    chip_pairs = [(i, i ^ CHIP) for i in range(streams)]
    core_pairs = [(i, i ^ 1) for i in range(streams)]
    relay = [
        (l * streams + g, (l + 1) % layers * streams + (g ^ (WRAP if l % 4 == 3 else HOP)))
        for l in range(layers)
        for g in range(streams)
    ]
    current = [entry[OFFSETS[k] : OFFSETS[k] + SIZES[k]].astype(BF) for k in range(CHUNKS)]
    for beat in range(beats):
        last = beat == beats - 1
        across = [lax.ppermute(part, "group", chip_pairs) for part in current]
        ready = lax.optimization_barrier((*current, *[across[k] for k in GATE]))
        beside = [
            lax.ppermute((ready if k in GATED else current)[k], "group", core_pairs) for k in range(CHUNKS)
        ]
        settled = list(across)
        for k, part in zip(GATE, ready[CHUNKS:]):
            settled[k] = part
        corner = [lax.ppermute(part, "group", core_pairs) for part in settled]
        parts = [part for group_parts in zip(current, beside, across, corner) for part in group_parts]
        where = [(i, k) for k in range(CHUNKS) for i in (0, 1, CHIP, CHIP ^ 1)]

        def call(chunks, parts, hist):
            operands = [scal, sched, hist, tile_set, *weights, *parts]
            from_input = beat == 0 and parts
            first = HBM if from_input else VMEM
            specs = [SMEM] * 2 + [first] * 6 + [VMEM] * len(parts)
            scratch = [
                pltpu.VMEM((pairs, tb, width), F32),
                pltpu.VMEM((nb, tb, width), BF),
                pltpu.SemaphoreType.DMA((8,)),
            ]
            if beat == 0:
                operands.append(staged)
                specs.append(first)
            alias = {}
            share = sum(SIZES[k] for k in chunks)
            if last:
                shapes = [
                    jax.ShapeDtypeStruct((nb, tb, width), F32),
                    jax.ShapeDtypeStruct((blocks, tb, width), BF),
                ]
                out_specs = [VMEM, ANY]
            else:
                operands.append(feed)
                specs.append(ANY)
                scratch.append(pltpu.VMEM((share, tb, width), F32))
                shapes = [jax.ShapeDtypeStruct((SIZES[k], tb, width), BF) for k in chunks]
                if parts:
                    shapes.append(pltpu.VMEM((blocks, tb, width), BF))
                    alias = {} if from_input else {2: len(chunks)}
                if from_input:
                    shapes += [pltpu.VMEM(x.shape, x.dtype) for x in kept]
                out_specs = [VMEM] * len(shapes)
            return pl.pallas_call(
                functools.partial(beat_kernel, beat, last, nb, pairs, where if parts else [], chunks),
                out_shape=shapes,
                in_specs=specs,
                out_specs=out_specs,
                input_output_aliases=alias,
                scratch_shapes=scratch,
                compiler_params=pltpu.CompilerParams(**PARAMS),
                cost_estimate=pl.CostEstimate(
                    flops=share * COST, bytes_accessed=share * 1_000_000, transcendentals=share * 65536
                ),
            )(*operands)

        if last:
            result, history = call(list(range(CHUNKS)), parts, hist)
        else:
            front, hist, *handed = call([0], parts, hist)
            if beat == 0:
                tile_set, *weights, staged = handed
            outs = [front, *call(list(range(1, CHUNKS)), [], hist)]
            current = [lax.ppermute(part, ("layer", "group"), relay) for part in outs]
    return (
        result.reshape(1, 1, rows, width),
        history.reshape(1, blocks * tb, width),
    )


def solution(mesh):
    return jax.shard_map(
        local,
        mesh=mesh,
        in_specs=(
            P("layer", "group", None, None),
            P("group", None, None, None),
            P(),
            P(),
            P("group", None, None, None),
            P("group", None),
            P("group", None),
            P("layer", None, None),
            P("layer", None, None),
            P("layer", None),
            P("layer", None, None),
            P("layer", None, None),
        ),
        out_specs=(P("layer", "group", None, None), P("layer", None, None)),
        check_vma=False,
    )
```
